32 devices in a mesh: dp: 8 (over y, x, core), head: 4 (over z).
Axes of the slice: x: 2, y: 2, z: 4, core: 2. Of those that a mesh axis runs over, the one named last changes fastest.
Arguments:
- queries: bfloat16 [3072, 512], P('dp', 'head'), may hold values from -8 to 8
- keys: bfloat16 [3072, 128], P('dp'), may hold values from -5 to 5
- values: bfloat16 [3072, 128], P('dp'), may hold values from -6 to 6
- block_of_slot: int32 [16], replicated, may hold values from 0 to 15, as said below
- doc_lengths: int32 [4], replicated, may hold values from 1 to 1536, 3072 in all
- out_weight: bfloat16 [512, 2048], P('head'), may hold values from -0.5 to 0.5
Outputs:
- mixed: bfloat16 [3072, 2048], P(('dp', 'head'))
The draws below stay inside these ranges and needn't reach their ends.
Inputs may be any that keep to these rules, and one draw needn't show every extreme that they name: `block_of_slot`: a permutation of 0 .. 15; entries 2 i and 2 i + 1 are the two slots of index i of dp, and they add to 15.
All inputs are finite; a program needn't handle non-finite values.
Results may differ from the reference program's by a relative error of at most 0.02.
Values may be sent and summed in bfloat16 or wider, within the bound.
A program may use at most 64 MiB of HBM per device.

```python
import math
import jax
import jax.numpy as jnp
import numpy as np
from jax import lax

D = 2048
HD = 128
QHEADS = 4
GROUP = 4
KVH = 1
TOK_DEV = 384
HALF = 192
TOKENS = 3072
BLOCKS = 16
DOCS = 4


def shared_draw(key):
    base = jax.random.fold_in(key, 7)
    key_vals = jnp.clip(jax.random.normal(jax.random.fold_in(base, 5), (TOKENS, KVH, HD), jnp.float32), -4.0, 4.0)
    query_vals = 1.5 * jnp.clip(jax.random.normal(jax.random.fold_in(base, 6), (TOKENS, QHEADS, HD), jnp.float32), -4.0, 4.0)
    return (query_vals.reshape(TOKENS, QHEADS * HD), key_vals.reshape(TOKENS, KVH * HD))


def draw_queries(key, part):
    return shared_draw(key)[0].astype(jnp.bfloat16)


def draw_keys(key, part):
    return shared_draw(key)[1].astype(jnp.bfloat16)


def draw_block_of_slot(key, part):
    order = jax.random.permutation(jax.random.fold_in(key, 11), BLOCKS // 2)
    table = jnp.stack([order, BLOCKS - 1 - order], axis=1).reshape(BLOCKS)
    return table.astype(jnp.int32)


def block_scale(stream_key, extent, pieces, least, top_value):
    gain, own = 1.0, jax.random.fold_in(stream_key, 6)
    for position, parts in pieces:
        heights = jnp.exp(jax.random.uniform(jax.random.fold_in(own, position), (parts,), jnp.float32, least / len(pieces), top_value / len(pieces)))
        gain = gain * jnp.repeat(heights, extent[position] // parts).reshape([-1 if axis == position else 1 for axis in range(len(extent))])
    return gain


def split_up(amount, total, reach, slope):
    weights = [(1 << 20) // math.isqrt(standing ** slope) + 1 for standing in range(2, amount + 1)]
    surplus, given = total - reach - (amount - 1), [1] * (amount - 1)
    while surplus > 0:
        movable = [i for i in range(amount - 1) if given[i] < reach]
        mass, budget = sum([weights[i] for i in movable]), surplus
        for i in movable:
            extra = min(reach - given[i], max(1, budget * weights[i] // mass), surplus)
            given[i] = given[i] + extra
            surplus = surplus - extra
    return np.array([reach] + given)


def ragged_sizes(own_key, count, total, most, slope):
    if count == 2:
        one = jax.random.randint(own_key, (), max(1, total - most), min(most, total - 1) + 1)
        return jnp.stack([one, total - one])
    lengths = jnp.asarray(split_up(count, total, most, slope), jnp.int32)
    couples = (count - 1) // 2
    giver, sink = lengths[1:1 + 2 * couples:2], lengths[2:2 + 2 * couples:2]
    margin = jnp.minimum(giver - 1, most - sink)
    shifted = jax.random.randint(jax.random.fold_in(own_key, 1), (couples,), 0, 1 << 20) % (margin + 1)
    lengths = lengths.at[1:1 + 2 * couples:2].set(giver - shifted).at[2:2 + 2 * couples:2].set(sink + shifted)
    return lengths[jax.random.permutation(jax.random.fold_in(own_key, 2), count)]


def noise(key, shape, scale, most, cuts=(), kind=jnp.bfloat16):
    entries = scale * jax.random.normal(key, shape, jnp.float32)
    if cuts:
        entries = entries * block_scale(key, shape, cuts, -0.22, 0.18)
    return jnp.clip(entries, -most, most).astype(kind)


def setup_inputs(seed: int = 0) -> dict:
    key_of = jax.random.split(jax.random.key(seed), 7)
    return {
        "queries": draw_queries(jax.random.fold_in(key_of[6], 71), 0),
        "keys": draw_keys(jax.random.fold_in(key_of[6], 71), 0),
        "values": noise(key_of[2], (TOKENS, KVH * HD), 1.0, 6.0, ((0, 8),)),
        "block_of_slot": draw_block_of_slot(jax.random.fold_in(key_of[6], 71), 0),
        "doc_lengths": ragged_sizes(key_of[4], DOCS, TOKENS, TOKENS // 2, 2).astype(jnp.int32),
        "out_weight": noise(key_of[5], (QHEADS * HD, D), HD ** -0.5, 0.5, ((0, 4),)),
    }


def reference(queries, keys, values, block_of_slot, doc_lengths, out_weight):
    row_index = jnp.arange(TOKENS, dtype=jnp.int32)
    positions = block_of_slot[row_index // HALF] * HALF + row_index % HALF
    bounds = jnp.cumsum(doc_lengths)[:-1]
    documents = lax.optimization_barrier(jnp.sum((positions[:, None] >= bounds[None, :]).astype(jnp.int32), axis=1))
    score_scale = 1.0 / math.sqrt(HD)
    block_count = TOKENS // TOK_DEV
    query_blocks = queries.reshape(block_count, TOK_DEV, QHEADS * HD)
    pos_blocks = positions.reshape(block_count, TOK_DEV)
    doc_blocks = documents.reshape(block_count, TOK_DEV)

    def one_head(head_index):
        kv_start = head_index // GROUP * HD
        head_keys = lax.dynamic_slice_in_dim(keys, kv_start, HD, 1)
        head_values = lax.dynamic_slice_in_dim(values, kv_start, HD, 1)

        def one_block(inputs):
            query_rows, query_pos, query_doc = inputs
            head_queries = lax.dynamic_slice_in_dim(query_rows, head_index * HD, HD, 1)
            scores = jnp.dot(head_queries, head_keys.T, preferred_element_type=jnp.float32) * score_scale
            allowed = (query_doc[:, None] == documents[None, :]) & (positions[None, :] <= query_pos[:, None])
            masked = jnp.where(allowed, scores, -jnp.inf)
            row_max = lax.optimization_barrier(jnp.max(masked, axis=1, keepdims=True))
            weights = jnp.where(allowed, jnp.exp(masked - row_max), 0.0)
            numerator = jnp.dot(weights.astype(jnp.bfloat16), head_values, preferred_element_type=jnp.float32)
            return (numerator / lax.optimization_barrier(jnp.sum(weights, axis=1, keepdims=True))).astype(jnp.bfloat16)
        return lax.map(one_block, (query_blocks, pos_blocks, doc_blocks))
    attended = lax.map(one_head, jnp.arange(QHEADS, dtype=jnp.int32))
    attended = attended.transpose(1, 2, 0, 3).reshape(TOKENS, QHEADS * HD)

    def add_head(total, head_index):
        head_cols = lax.dynamic_slice_in_dim(attended, head_index * HD, HD, 1)
        head_rows = lax.dynamic_slice_in_dim(out_weight, head_index * HD, HD, 0)
        term = jnp.dot(head_cols, head_rows, preferred_element_type=jnp.float32)
        rounded = lax.optimization_barrier(term.astype(jnp.bfloat16))
        return (total + rounded.astype(jnp.float32), None)
    total, _ = lax.scan(add_head, jnp.zeros((TOKENS, D), jnp.float32), jnp.arange(QHEADS, dtype=jnp.int32))
    return total.astype(jnp.bfloat16)
```

```python
import functools
import math

import jax
import jax.numpy as jnp
from jax import lax
from jax.experimental import pallas as pl
from jax.experimental.pallas import tpu as pltpu
from jax.sharding import PartitionSpec as P

MESH = pl.DeviceIdType.MESH
NEG = -1e30


def slot_positions(first_row, row_count, table, half_rows):
    row_index = first_row + jnp.arange(row_count, dtype=jnp.int32)
    slot_index = row_index // half_rows
    all_slots = jnp.arange(table.shape[0], dtype=jnp.int32)
    block_id = jnp.sum(
        jnp.where(slot_index[:, None] == all_slots[None, :], table[None, :], 0), axis=1
    )
    return block_id * half_rows + row_index % half_rows


def document_ids(positions, bounds):
    return jnp.sum((positions[:, None] >= bounds[None, :]).astype(jnp.int32), axis=1)


def general(queries, keys, values, block_of_slot, doc_lengths, out_weight):
    tok_rows = queries.shape[0]
    head_size = queries.shape[1]
    half_rows = tok_rows // 2
    head_total = lax.axis_size("head")
    group_size = min(8, head_total)
    kv_start = lax.axis_index("head") // group_size * head_size
    own_keys = lax.dynamic_slice_in_dim(keys, kv_start, head_size, 1)
    own_values = lax.dynamic_slice_in_dim(values, kv_start, head_size, 1)
    count = doc_lengths.shape[0]
    before = jnp.arange(count)[None, :] <= jnp.arange(count - 1)[:, None]
    bounds = jnp.sum(jnp.where(before, doc_lengths[None, :], 0), axis=1)
    query_pos = slot_positions(lax.axis_index("dp") * tok_rows, tok_rows, block_of_slot, half_rows)
    query_doc = document_ids(query_pos, bounds)
    score_scale = 1.0 / math.sqrt(head_size)

    def attend(totals, key_block, value_block, allowed):
        run_max, run_sum, run_acc = totals
        scores = (
            jnp.einsum("qd,kd->qk", queries, key_block, preferred_element_type=jnp.float32)
            * score_scale
        )
        masked = jnp.where(allowed, scores, NEG)
        new_max = jnp.maximum(run_max, jnp.max(masked, axis=1))
        weights = jnp.where(allowed, jnp.exp(masked - new_max[:, None]), 0.0)
        factor = jnp.exp(run_max - new_max)
        new_sum = run_sum * factor + jnp.sum(weights, axis=1)
        new_acc = run_acc * factor[:, None] + jnp.dot(
            weights.astype(jnp.bfloat16), value_block, preferred_element_type=jnp.float32
        )
        return (new_max, new_sum, new_acc)

    totals = (
        jnp.full((tok_rows,), NEG, jnp.float32),
        jnp.zeros((tok_rows,), jnp.float32),
        jnp.zeros((tok_rows, head_size), jnp.float32),
    )
    key_piece = lax.all_gather(own_keys, "dp", axis=0, tiled=True)
    value_piece = lax.all_gather(own_values, "dp", axis=0, tiled=True)
    shard_count = key_piece.shape[0] // tok_rows
    per_step = max(
        [1]
        + [
            option_width
            for option_width in range(1, shard_count + 1)
            if shard_count % option_width == 0 and option_width * tok_rows <= 1536
        ]
    )
    step_rows = per_step * tok_rows
    step_count = shard_count // per_step
    key_blocks = key_piece.reshape(step_count, step_rows, head_size)
    value_blocks = value_piece.reshape(step_count, step_rows, head_size)
    step_starts = step_rows * jnp.arange(step_count, dtype=jnp.int32)

    def advance(running, inputs):
        key_block, value_block, block_start = inputs
        key_pos = slot_positions(block_start, step_rows, block_of_slot, half_rows)
        key_doc = document_ids(key_pos, bounds)
        allowed = (query_doc[:, None] == key_doc[None, :]) & (
            key_pos[None, :] <= query_pos[:, None]
        )
        running = lax.cond(
            jnp.any(allowed),
            lambda held: attend(held, key_block, value_block, allowed),
            lambda held: held,
            running,
        )
        return (running, None)

    totals, _ = lax.scan(advance, totals, (key_blocks, value_blocks, step_starts))
    run_max, run_sum, run_acc = totals
    attended = (run_acc / run_sum[:, None]).astype(jnp.bfloat16)
    partial_terms = jnp.dot(attended, out_weight, preferred_element_type=jnp.float32)
    return lax.psum_scatter(
        partial_terms.astype(jnp.bfloat16), "head", scatter_dimension=0, tiled=True
    )


def flip(index, bit):
    return index + bit - 2 * bit * lax.rem(lax.div(index, bit), 2)


def flipped(index, mask):
    bit = 1
    while bit <= mask:
        if mask & bit:
            index = flip(index, bit)
        bit *= 2
    return index


CORE, ALONG_X, ALONG_Y = 1, 2, 4
DIAG = ALONG_X + ALONG_Y


def fused_kernel(
    dp_total, head_total, table, lengths, q_in, k_in, v_in, w_in, out_ref,
    q_buf, k_buf, v_buf, w_buf, att_buf,
    local_sem, q_send, q_recv, k_send, k_recv, v_send, v_recv, z_send, z_recv, w_send, w_recv,
):
    me, head = lax.axis_index("dp"), lax.axis_index("head")
    rows, head_size = q_buf.shape[1:]
    tok_rows = k_buf.shape[1]
    half_rows = tok_rows // 2
    width = w_buf.shape[-1]
    near = {mask: flipped(me, mask) for mask in range(dp_total)}
    heads = {mask: flipped(head, mask) for mask in range(head_total)}

    barrier = pltpu.get_barrier_semaphore()
    for mask in (CORE, ALONG_X, ALONG_Y):
        pl.semaphore_signal(barrier, inc=1, device_id=(near[mask], head), device_id_type=MESH)
    for mask in range(1, head_total):
        pl.semaphore_signal(barrier, inc=1, device_id=(me, heads[mask]), device_id_type=MESH)

    def own_rows(of_head):
        return q_in.at[pl.ds(pl.multiple_of(of_head * rows, 16), rows)]

    locals_ = [
        pltpu.make_async_copy(k_in, k_buf.at[0], local_sem.at[0]),
        pltpu.make_async_copy(v_in, v_buf.at[0], local_sem.at[1]),
        pltpu.make_async_copy(own_rows(head), q_buf.at[0], local_sem.at[2]),
        pltpu.make_async_copy(w_in, w_buf.at[0], local_sem.at[3]),
    ]
    for copy in locals_:
        copy.start()
    pl.semaphore_wait(barrier, 3 + head_total - 1)

    sent = []

    def send(src, dst, send_sem, recv_sem, to):
        copy = pltpu.make_async_remote_copy(
            src_ref=src, dst_ref=dst, send_sem=send_sem, recv_sem=recv_sem,
            device_id=to, device_id_type=MESH,
        )
        copy.start()
        sent.append(copy)

    def arrived(dst, recv_sem):
        pltpu.make_async_remote_copy(
            src_ref=dst, dst_ref=dst, send_sem=recv_sem, recv_sem=recv_sem,
            device_id=(near[CORE], head), device_id_type=MESH,
        ).wait_recv()

    def pass_on(buf, send_sems, recv_sems, slot, mask, src=None):
        landing = slot ^ mask
        number = landing * 3 + (CORE, ALONG_X, ALONG_Y).index(mask)
        send(
            buf.at[slot] if src is None else src, buf.at[landing],
            send_sems.at[number], recv_sems.at[landing], (near[mask], head),
        )

    def k_pass(slot, mask, src=None):
        pass_on(k_buf, k_send, k_recv, slot, mask, src)

    def v_pass(slot, mask, src=None):
        pass_on(v_buf, v_send, v_recv, slot, mask, src)

    def k_wait(slot):
        arrived(k_buf.at[slot], k_recv.at[slot])

    def v_wait(slot):
        arrived(v_buf.at[slot], v_recv.at[slot])

    def w_part(origin, half):
        columns = pl.ds(0, width) if half is None else pl.ds(half * (width // 2), width // 2)
        return w_buf.at[pl.ds(1, head_total - 1), near[origin], :, columns]

    def w_number(origin, half):
        return origin if origin & DIAG != DIAG else dp_total + 2 * (origin & 1) + half

    def w_pass(slot, mask, half=None):
        landing = slot ^ mask
        number = w_number(landing, half)
        send(
            w_part(slot, half), w_part(slot, half),
            w_send.at[number * 3 + (CORE, ALONG_X, ALONG_Y).index(mask)], w_recv.at[number],
            (near[mask], head),
        )

    def w_wait(slot, half=None):
        arrived(w_part(slot, half), w_recv.at[w_number(slot, half)])

    for mask in range(1, head_total):
        send(own_rows(heads[mask]), q_buf.at[mask], q_send.at[mask], q_recv.at[mask], (me, heads[mask]))
    k_pass(0, ALONG_X, k_in)
    v_pass(0, ALONG_Y, v_in)
    for mask in range(1, head_total):
        send(w_in.at[me], w_buf.at[mask, me], z_send.at[mask], z_recv.at[mask], (me, heads[mask]))
    v_pass(0, ALONG_X, v_in)
    k_pass(0, ALONG_Y, k_in)
    k_pass(0, CORE, k_in)
    v_pass(0, CORE, v_in)

    first_slot = me * 2 + lax.div(head * rows, half_rows)
    first_pos = table[first_slot] * half_rows + lax.rem(head * rows, half_rows)
    query_pos = first_pos + lax.broadcasted_iota(jnp.int32, (rows, 1), 0)
    low = jnp.zeros((rows, 1), jnp.int32)
    bound = jnp.int32(0)
    for i in range(lengths.shape[0] - 1):
        bound = bound + lengths[i]
        low = jnp.where(query_pos >= bound, bound, low)
    lane = lax.broadcasted_iota(jnp.int32, (1, tok_rows), 1)
    exponent = math.log2(math.e) / math.sqrt(head_size)
    total_rows = head_total * rows

    def scores_of(slot):
        start0 = table[near[slot] * 2] * half_rows
        start1 = table[near[slot] * 2 + 1] * half_rows - half_rows
        key_pos = lane + jnp.where(lane < half_rows, start0, start1)
        allowed = (key_pos <= query_pos) & (key_pos >= low)
        scores = lax.dot_general(
            q_buf[...].reshape(total_rows, head_size), k_buf[slot],
            (((1,), (1,)), ((), ())), preferred_element_type=jnp.float32,
        ).reshape(head_total, rows, tok_rows)
        return jnp.where(allowed[None], scores, NEG).reshape(total_rows, tok_rows)

    def fold(totals, slot):
        masked = scores_of(slot)
        top = jnp.max(masked, axis=1, keepdims=True)
        new_max = top if totals is None else jnp.maximum(totals[0], top)
        weights = jnp.exp2((masked - new_max) * exponent)
        added = jnp.sum(weights, axis=1, keepdims=True)
        product = jnp.dot(weights.astype(jnp.bfloat16), v_buf[slot], preferred_element_type=jnp.float32)
        if totals is None:
            return new_max, added, product
        factor = jnp.exp2((totals[0] - new_max) * exponent)
        return new_max, totals[1] * factor + added, totals[2] * factor + product

    k_wait(ALONG_X)
    k_pass(ALONG_X, ALONG_Y)
    k_pass(ALONG_X, CORE)
    v_wait(ALONG_Y)
    v_pass(ALONG_Y, ALONG_X)
    v_pass(ALONG_Y, CORE)
    for mask in range(1, head_total):
        arrived(w_buf.at[mask, me], z_recv.at[mask])
    w_pass(0, ALONG_X)
    w_pass(0, ALONG_Y)
    w_pass(0, CORE)
    v_wait(ALONG_X)
    v_pass(ALONG_X, CORE)
    k_wait(ALONG_Y)
    k_pass(ALONG_Y, CORE)
    for copy in locals_:
        copy.wait()
    for mask in range(1, head_total):
        arrived(q_buf.at[mask], q_recv.at[mask])
    totals = fold(None, 0)
    k_wait(DIAG)
    k_pass(DIAG, CORE)
    v_wait(DIAG)
    v_pass(DIAG, CORE)
    totals = fold(totals, ALONG_X)
    w_wait(ALONG_X)
    w_pass(ALONG_X, ALONG_Y, 0)
    w_pass(ALONG_X, CORE)
    w_wait(ALONG_Y)
    w_pass(ALONG_Y, ALONG_X, 1)
    w_pass(ALONG_Y, CORE)
    totals = fold(totals, ALONG_Y)
    for slot in (CORE, CORE + ALONG_X, CORE + ALONG_Y):
        k_wait(slot)
        v_wait(slot)
        totals = fold(totals, slot)
    for half in (0, 1):
        w_wait(DIAG, half)
        w_pass(DIAG, CORE, half)
    totals = fold(totals, DIAG)
    k_wait(CORE + DIAG)
    v_wait(CORE + DIAG)
    _, run_sum, run_acc = fold(totals, CORE + DIAG)
    attended = (run_acc / run_sum).astype(jnp.bfloat16)
    for mask in range(head_total):
        att_buf[:, mask * head_size : (mask + 1) * head_size] = attended[mask * rows : (mask + 1) * rows]
    w_wait(CORE)
    w_wait(CORE + ALONG_X)
    w_wait(CORE + ALONG_Y)
    w_wait(CORE + DIAG, 0)
    w_wait(CORE + DIAG, 1)
    step = min(width, 512)
    for start in range(0, width, step):
        block = w_buf[:, :, :, start : start + step].reshape(head_total * head_size, step)
        out_ref[:, start : start + step] = jnp.dot(
            att_buf[...], block, preferred_element_type=jnp.float32
        ).astype(out_ref.dtype)
    for copy in sent:
        copy.wait_send()


def fused(dp_total, head_total, queries, keys, values, block_of_slot, doc_lengths, out_weight):
    tok_rows, head_size = queries.shape
    rows = tok_rows // head_total
    depth, width = out_weight.shape
    any_, smem, vmem = (pl.BlockSpec(memory_space=m) for m in (pl.ANY, pltpu.SMEM, pltpu.VMEM))
    dma = pltpu.SemaphoreType.DMA
    piece = depth // dp_total
    return pl.pallas_call(
        functools.partial(fused_kernel, dp_total, head_total),
        out_shape=jax.ShapeDtypeStruct((rows, width), jnp.bfloat16),
        in_specs=[smem, smem, any_, any_, any_, any_],
        out_specs=vmem,
        scratch_shapes=[
            pltpu.VMEM((head_total, rows, head_size), jnp.bfloat16),
            pltpu.VMEM((dp_total, tok_rows, head_size), jnp.bfloat16),
            pltpu.VMEM((dp_total, tok_rows, head_size), jnp.bfloat16),
            pltpu.VMEM((head_total, dp_total, piece, width), jnp.bfloat16),
            pltpu.VMEM((rows, head_total * head_size), jnp.bfloat16),
            dma((4,)),
            dma((head_total,)),
            dma((head_total,)),
            dma((3 * dp_total,)),
            dma((dp_total,)),
            dma((3 * dp_total,)),
            dma((dp_total,)),
            dma((head_total,)),
            dma((head_total,)),
            dma((3 * (dp_total + 4),)),
            dma((dp_total + 4,)),
        ],
        compiler_params=pltpu.CompilerParams(
            collective_id=0, has_side_effects=True, vmem_limit_bytes=48 * 2**20
        ),
        cost_estimate=pl.CostEstimate(
            flops=4 * tok_rows * tok_rows * dp_total * head_size + 2 * rows * head_total * depth * width,
            bytes_accessed=2 * (rows * width + depth * width + 3 * tok_rows * head_size),
            transcendentals=tok_rows * tok_rows * dp_total,
        ),
    )(
        block_of_slot, doc_lengths, queries, keys, values,
        out_weight.reshape(dp_total, piece, width),
    )


def solution(mesh):
    dp_total, head_total = mesh.shape["dp"], mesh.shape["head"]

    def per_device(queries, keys, values, block_of_slot, doc_lengths, out_weight):
        tok_rows, head_size = queries.shape
        rows = tok_rows // head_total
        fits = (
            dp_total == 2 ** 3
            and head_total & (head_total - 1) == 0
            and keys.shape[1] == head_size
            and rows % 16 == 0
            and (tok_rows // 2) % rows == 0
            and out_weight.shape[0] % (16 * dp_total) == 0
            and out_weight.shape[0] == head_size
        )
        run = functools.partial(fused, dp_total, head_total) if fits else general
        return run(queries, keys, values, block_of_slot, doc_lengths, out_weight)

    return jax.shard_map(
        per_device,
        mesh=mesh,
        in_specs=(P("dp", "head"), P("dp", None), P("dp", None), P(), P(), P("head", None)),
        out_specs=P(("dp", "head"), None),
        check_vma=False,
    )
```

```python
import functools
import math

import jax
import jax.numpy as jnp
from jax import lax
from jax.experimental import pallas as pl
from jax.experimental.pallas import tpu as pltpu
from jax.sharding import PartitionSpec as P

MESH = pl.DeviceIdType.MESH
NEG = -1e30


def slot_positions(first_row, row_count, table, half_rows):
    row_index = first_row + jnp.arange(row_count, dtype=jnp.int32)
    slot_index = row_index // half_rows
    all_slots = jnp.arange(table.shape[0], dtype=jnp.int32)
    block_id = jnp.sum(
        jnp.where(slot_index[:, None] == all_slots[None, :], table[None, :], 0), axis=1
    )
    return block_id * half_rows + row_index % half_rows


def document_ids(positions, bounds):
    return jnp.sum((positions[:, None] >= bounds[None, :]).astype(jnp.int32), axis=1)


def general(queries, keys, values, block_of_slot, doc_lengths, out_weight):
    tok_rows = queries.shape[0]
    head_size = queries.shape[1]
    half_rows = tok_rows // 2
    head_total = lax.axis_size("head")
    group_size = min(8, head_total)
    kv_start = lax.axis_index("head") // group_size * head_size
    own_keys = lax.dynamic_slice_in_dim(keys, kv_start, head_size, 1)
    own_values = lax.dynamic_slice_in_dim(values, kv_start, head_size, 1)
    count = doc_lengths.shape[0]
    before = jnp.arange(count)[None, :] <= jnp.arange(count - 1)[:, None]
    bounds = jnp.sum(jnp.where(before, doc_lengths[None, :], 0), axis=1)
    query_pos = slot_positions(lax.axis_index("dp") * tok_rows, tok_rows, block_of_slot, half_rows)
    query_doc = document_ids(query_pos, bounds)
    score_scale = 1.0 / math.sqrt(head_size)

    def attend(totals, key_block, value_block, allowed):
        run_max, run_sum, run_acc = totals
        scores = (
            jnp.einsum("qd,kd->qk", queries, key_block, preferred_element_type=jnp.float32)
            * score_scale
        )
        masked = jnp.where(allowed, scores, NEG)
        new_max = jnp.maximum(run_max, jnp.max(masked, axis=1))
        weights = jnp.where(allowed, jnp.exp(masked - new_max[:, None]), 0.0)
        factor = jnp.exp(run_max - new_max)
        new_sum = run_sum * factor + jnp.sum(weights, axis=1)
        new_acc = run_acc * factor[:, None] + jnp.dot(
            weights.astype(jnp.bfloat16), value_block, preferred_element_type=jnp.float32
        )
        return (new_max, new_sum, new_acc)

    totals = (
        jnp.full((tok_rows,), NEG, jnp.float32),
        jnp.zeros((tok_rows,), jnp.float32),
        jnp.zeros((tok_rows, head_size), jnp.float32),
    )
    key_piece = lax.all_gather(own_keys, "dp", axis=0, tiled=True)
    value_piece = lax.all_gather(own_values, "dp", axis=0, tiled=True)
    shard_count = key_piece.shape[0] // tok_rows
    per_step = max(
        [1]
        + [
            option_width
            for option_width in range(1, shard_count + 1)
            if shard_count % option_width == 0 and option_width * tok_rows <= 1536
        ]
    )
    step_rows = per_step * tok_rows
    step_count = shard_count // per_step
    key_blocks = key_piece.reshape(step_count, step_rows, head_size)
    value_blocks = value_piece.reshape(step_count, step_rows, head_size)
    step_starts = step_rows * jnp.arange(step_count, dtype=jnp.int32)

    def advance(running, inputs):
        key_block, value_block, block_start = inputs
        key_pos = slot_positions(block_start, step_rows, block_of_slot, half_rows)
        key_doc = document_ids(key_pos, bounds)
        allowed = (query_doc[:, None] == key_doc[None, :]) & (
            key_pos[None, :] <= query_pos[:, None]
        )
        running = lax.cond(
            jnp.any(allowed),
            lambda held: attend(held, key_block, value_block, allowed),
            lambda held: held,
            running,
        )
        return (running, None)

    totals, _ = lax.scan(advance, totals, (key_blocks, value_blocks, step_starts))
    run_max, run_sum, run_acc = totals
    attended = (run_acc / run_sum[:, None]).astype(jnp.bfloat16)
    partial_terms = jnp.dot(attended, out_weight, preferred_element_type=jnp.float32)
    return lax.psum_scatter(
        partial_terms.astype(jnp.bfloat16), "head", scatter_dimension=0, tiled=True
    )


def flip(index, bit):
    return index + bit - 2 * bit * lax.rem(lax.div(index, bit), 2)


def flipped(index, mask):
    bit = 1
    while bit <= mask:
        if mask & bit:
            index = flip(index, bit)
        bit *= 2
    return index


CORE, ALONG_X, ALONG_Y = 1, 2, 4
DIAG = ALONG_X + ALONG_Y


def fused_kernel(
    dp_total, head_total, shared, table, lengths, q_in, k_in, v_in, w_in, out_ref,
    q_buf, k_buf, v_buf, w_buf, att_buf,
    local_sem, q_send, q_recv, k_send, k_recv, v_send, v_recv, z_send, z_recv, w_send, w_recv, s_send, s_recv,
):
    me, head = lax.axis_index("dp"), lax.axis_index("head")
    rows, head_size = q_buf.shape[1:]
    tok_rows = k_buf.shape[1]
    half_rows = tok_rows // 2
    depth, width = w_buf.shape[1:]
    piece = width // dp_total
    near = {mask: flipped(me, mask) for mask in range(dp_total)}
    heads = {mask: flipped(head, mask) for mask in range(head_total)}

    barrier = pltpu.get_barrier_semaphore()
    for mask in (CORE, ALONG_X, ALONG_Y):
        pl.semaphore_signal(barrier, inc=1, device_id=(near[mask], head), device_id_type=MESH)
    for mask in range(1, head_total):
        pl.semaphore_signal(barrier, inc=1, device_id=(me, heads[mask]), device_id_type=MESH)

    def own_rows(of_head):
        return q_in.at[pl.ds(pl.multiple_of(of_head * rows, 16), rows)]

    locals_ = [
        pltpu.make_async_copy(k_in, k_buf.at[0], local_sem.at[0]),
        pltpu.make_async_copy(v_in, v_buf.at[0], local_sem.at[1]),
        pltpu.make_async_copy(own_rows(head), q_buf.at[0], local_sem.at[2]),
        pltpu.make_async_copy(w_in, w_buf.at[0], local_sem.at[3]),
    ]
    for copy in locals_:
        copy.start()
    pl.semaphore_wait(barrier, 3 + head_total - 1)

    sent = []

    def send(src, dst, send_sem, recv_sem, to):
        copy = pltpu.make_async_remote_copy(
            src_ref=src, dst_ref=dst, send_sem=send_sem, recv_sem=recv_sem,
            device_id=to, device_id_type=MESH,
        )
        copy.start()
        sent.append(copy)

    def arrived(dst, recv_sem):
        pltpu.make_async_remote_copy(
            src_ref=dst, dst_ref=dst, send_sem=recv_sem, recv_sem=recv_sem,
            device_id=(near[CORE], head), device_id_type=MESH,
        ).wait_recv()

    def pass_on(buf, send_sems, recv_sems, slot, mask, src=None):
        landing = slot ^ mask
        number = landing * 3 + (CORE, ALONG_X, ALONG_Y).index(mask)
        send(
            buf.at[slot] if src is None else src, buf.at[landing],
            send_sems.at[number], recv_sems.at[landing], (near[mask], head),
        )

    def k_pass(slot, mask, src=None):
        pass_on(k_buf, k_send, k_recv, slot, mask, src)

    def v_pass(slot, mask, src=None):
        pass_on(v_buf, v_send, v_recv, slot, mask, src)

    def k_wait(slot):
        arrived(k_buf.at[slot], k_recv.at[slot])

    def v_wait(slot):
        arrived(v_buf.at[slot], v_recv.at[slot])

    def columns_of(origin):
        return pl.ds(pl.multiple_of(near[origin] * piece, 128), piece)

    def w_part(foreign, origin, half):
        span = pl.ds(0, shared) if half is None else pl.ds(half * (shared // 2), shared // 2)
        return w_buf.at[foreign, span, columns_of(origin)]

    def w_number(origin, half):
        return origin if origin & DIAG != DIAG else dp_total + 2 * (origin & 1) + (half or 0)

    def w_pass(foreign, slot, mask, half=None):
        number = w_number(slot ^ mask, half)
        send(
            w_part(foreign, slot, half), w_part(foreign, slot, half),
            w_send.at[foreign, number * 3 + (CORE, ALONG_X, ALONG_Y).index(mask)],
            w_recv.at[foreign, number], (near[mask], head),
        )

    def w_wait(foreign, slot, half=None):
        arrived(w_part(foreign, slot, half), w_recv.at[foreign, w_number(slot, half)])

    def straight(of_core):
        half_span = (depth - shared) // 2
        return pl.ds(pl.multiple_of(shared + of_core * half_span, 16), half_span)

    def straight_to_core(foreign):
        part = w_buf.at[foreign, straight(lax.rem(me, 2))]
        arrived(part, s_recv.at[0, foreign])
        send(part, part, s_send.at[1, foreign], s_recv.at[1, foreign], (near[CORE], head))

    k_pass(0, ALONG_X, k_in)
    v_pass(0, ALONG_Y, v_in)
    for mask in range(1, head_total):
        send(
            w_in.at[pl.ds(0, shared), columns_of(0)], w_part(mask, 0, None),
            z_send.at[mask], z_recv.at[mask], (me, heads[mask]),
        )
    v_pass(0, ALONG_X, v_in)
    k_pass(0, ALONG_Y, k_in)
    k_pass(0, CORE, k_in)
    v_pass(0, CORE, v_in)
    for mask in range(1, head_total):
        send(own_rows(heads[mask]), q_buf.at[mask], q_send.at[mask], q_recv.at[mask], (me, heads[mask]))
    if shared < depth:
        span = straight(lax.rem(me, 2))
        for mask in range(1, head_total):
            send(
                w_in.at[span], w_buf.at[mask, span],
                s_send.at[0, mask], s_recv.at[0, mask], (me, heads[mask]),
            )

    first_slot = me * 2 + lax.div(head * rows, half_rows)
    first_pos = table[first_slot] * half_rows + lax.rem(head * rows, half_rows)
    query_pos = first_pos + lax.broadcasted_iota(jnp.int32, (rows, 1), 0)
    low = jnp.zeros((rows, 1), jnp.int32)
    bound = jnp.int32(0)
    for i in range(lengths.shape[0] - 1):
        bound = bound + lengths[i]
        low = jnp.where(query_pos >= bound, bound, low)
    lane = lax.broadcasted_iota(jnp.int32, (1, tok_rows), 1)
    exponent = math.log2(math.e) / math.sqrt(head_size)
    total_rows = head_total * rows

    def scores_of(slot):
        start0 = table[near[slot] * 2] * half_rows
        start1 = table[near[slot] * 2 + 1] * half_rows - half_rows
        key_pos = lane + jnp.where(lane < half_rows, start0, start1)
        allowed = (key_pos <= query_pos) & (key_pos >= low)
        scores = lax.dot_general(
            q_buf[...].reshape(total_rows, head_size), k_buf[slot],
            (((1,), (1,)), ((), ())), preferred_element_type=jnp.float32,
        ).reshape(head_total, rows, tok_rows)
        return jnp.where(allowed[None], scores, NEG).reshape(total_rows, tok_rows)

    def fold(totals, slot):
        masked = scores_of(slot)
        top = jnp.max(masked, axis=1, keepdims=True)
        new_max = top if totals is None else jnp.maximum(totals[0], top)
        weights = jnp.exp2((masked - new_max) * exponent)
        added = jnp.sum(weights, axis=1, keepdims=True)
        product = jnp.dot(weights.astype(jnp.bfloat16), v_buf[slot], preferred_element_type=jnp.float32)
        if totals is None:
            return new_max, added, product
        factor = jnp.exp2((totals[0] - new_max) * exponent)
        return new_max, totals[1] * factor + added, totals[2] * factor + product

    foreign_heads = range(1, head_total)

    def w_spread(foreign):
        arrived(w_part(foreign, 0, None), z_recv.at[foreign])
        for mask in (ALONG_X, ALONG_Y, CORE):
            w_pass(foreign, 0, mask)

    def w_second(foreign):
        w_wait(foreign, ALONG_X)
        w_pass(foreign, ALONG_X, ALONG_Y, 0)
        w_pass(foreign, ALONG_X, CORE)
        w_wait(foreign, ALONG_Y)
        w_pass(foreign, ALONG_Y, ALONG_X, 1)
        w_pass(foreign, ALONG_Y, CORE)

    def w_third(foreign):
        for half in (0, 1):
            w_wait(foreign, DIAG, half)
            w_pass(foreign, DIAG, CORE, half)

    k_wait(ALONG_X)
    k_pass(ALONG_X, ALONG_Y)
    k_pass(ALONG_X, CORE)
    v_wait(ALONG_Y)
    v_pass(ALONG_Y, ALONG_X)
    v_pass(ALONG_Y, CORE)
    w_spread(1)
    v_wait(ALONG_X)
    v_pass(ALONG_X, CORE)
    k_wait(ALONG_Y)
    k_pass(ALONG_Y, CORE)
    for foreign in foreign_heads[1:]:
        w_spread(foreign)
    k_wait(DIAG)
    k_pass(DIAG, CORE)
    v_wait(DIAG)
    v_pass(DIAG, CORE)
    for copy in locals_:
        copy.wait()
    for mask in foreign_heads:
        arrived(q_buf.at[mask], q_recv.at[mask])
    slots = [0, ALONG_X, ALONG_Y, CORE, CORE + ALONG_X, CORE + ALONG_Y, DIAG, CORE + DIAG]
    totals = None
    for slot in slots:
        if slot & CORE:
            k_wait(slot)
            v_wait(slot)
        totals = fold(totals, slot)
        number = slots.index(slot)
        if number % 2 and number // 2 < len(foreign_heads):
            w_second(foreign_heads[number // 2])
    for foreign in foreign_heads[(len(slots) // 2) :]:
        w_second(foreign)
    if shared < depth:
        for foreign in foreign_heads:
            straight_to_core(foreign)
    _, run_sum, run_acc = totals
    attended = (run_acc / run_sum).astype(jnp.bfloat16)
    for mask in range(head_total):
        att_buf[:, mask * head_size : (mask + 1) * head_size] = attended[mask * rows : (mask + 1) * rows]
    if shared < depth:
        for foreign in foreign_heads:
            arrived(w_buf.at[foreign, straight(1 - lax.rem(me, 2))], s_recv.at[1, foreign])

    def project(slot):
        columns = columns_of(slot)
        out_ref[:, columns] = jnp.dot(
            att_buf[...], w_buf[:, :, columns].reshape(head_total * depth, piece),
            preferred_element_type=jnp.float32,
        ).astype(out_ref.dtype)

    project(0)
    project(ALONG_X)
    project(ALONG_Y)
    for foreign in foreign_heads:
        w_third(foreign)
    for slot in (CORE, CORE + ALONG_X, CORE + ALONG_Y):
        for foreign in foreign_heads:
            w_wait(foreign, slot)
        project(slot)
    project(DIAG)
    for foreign in foreign_heads:
        w_wait(foreign, CORE + DIAG, 0)
        w_wait(foreign, CORE + DIAG, 1)
    project(CORE + DIAG)
    for copy in sent:
        copy.wait_send()


def fused(dp_total, head_total, queries, keys, values, block_of_slot, doc_lengths, out_weight):
    tok_rows, head_size = queries.shape
    rows = tok_rows // head_total
    depth, width = out_weight.shape
    any_, smem, vmem = (pl.BlockSpec(memory_space=m) for m in (pl.ANY, pltpu.SMEM, pltpu.VMEM))
    dma = pltpu.SemaphoreType.DMA
    shared = depth * 3 // 4 // 32 * 32
    return pl.pallas_call(
        functools.partial(fused_kernel, dp_total, head_total, shared),
        out_shape=jax.ShapeDtypeStruct((rows, width), jnp.bfloat16),
        in_specs=[smem, smem, any_, any_, any_, any_],
        out_specs=vmem,
        scratch_shapes=[
            pltpu.VMEM((head_total, rows, head_size), jnp.bfloat16),
            pltpu.VMEM((dp_total, tok_rows, head_size), jnp.bfloat16),
            pltpu.VMEM((dp_total, tok_rows, head_size), jnp.bfloat16),
            pltpu.VMEM((head_total, depth, width), jnp.bfloat16),
            pltpu.VMEM((rows, head_total * head_size), jnp.bfloat16),
            dma((4,)),
            dma((head_total,)),
            dma((head_total,)),
            dma((3 * dp_total,)),
            dma((dp_total,)),
            dma((3 * dp_total,)),
            dma((dp_total,)),
            dma((head_total,)),
            dma((head_total,)),
            dma((head_total, 3 * (dp_total + 4))),
            dma((head_total, dp_total + 4)),
            dma((2, head_total)),
            dma((2, head_total)),
        ],
        compiler_params=pltpu.CompilerParams(
            collective_id=0, has_side_effects=True, vmem_limit_bytes=60 * 2**20
        ),
        cost_estimate=pl.CostEstimate(
            flops=4 * tok_rows * tok_rows * dp_total * head_size + 2 * rows * head_total * depth * width,
            bytes_accessed=2 * (rows * width + depth * width + 3 * tok_rows * head_size),
            transcendentals=tok_rows * tok_rows * dp_total,
        ),
    )(
        block_of_slot, doc_lengths, queries, keys, values, out_weight,
    )


def solution(mesh):
    dp_total, head_total = mesh.shape["dp"], mesh.shape["head"]

    def per_device(queries, keys, values, block_of_slot, doc_lengths, out_weight):
        tok_rows, head_size = queries.shape
        rows = tok_rows // head_total
        fits = (
            dp_total == 2 ** 3
            and head_total & (head_total - 1) == 0
            and keys.shape[1] == head_size
            and rows % 16 == 0
            and (tok_rows // 2) % rows == 0
            and out_weight.shape[0] % 128 == 0
            and out_weight.shape[1] % (128 * dp_total) == 0
            and out_weight.shape[0] == head_size
        )
        run = functools.partial(fused, dp_total, head_total) if fits else general
        return run(queries, keys, values, block_of_slot, doc_lengths, out_weight)

    return jax.shard_map(
        per_device,
        mesh=mesh,
        in_specs=(P("dp", "head"), P("dp", None), P("dp", None), P(), P(), P("head", None)),
        out_specs=P(("dp", "head"), None),
        check_vma=False,
    )
```

```python
import functools
import math

import jax
import jax.numpy as jnp
from jax import lax
from jax.experimental import pallas as pl
from jax.experimental.pallas import tpu as pltpu
from jax.sharding import PartitionSpec as P

MESH = pl.DeviceIdType.MESH
NEG = -1e30


def slot_positions(first_row, row_count, table, half_rows):
    row_index = first_row + jnp.arange(row_count, dtype=jnp.int32)
    slot_index = row_index // half_rows
    all_slots = jnp.arange(table.shape[0], dtype=jnp.int32)
    block_id = jnp.sum(
        jnp.where(slot_index[:, None] == all_slots[None, :], table[None, :], 0), axis=1
    )
    return block_id * half_rows + row_index % half_rows


def document_ids(positions, bounds):
    return jnp.sum((positions[:, None] >= bounds[None, :]).astype(jnp.int32), axis=1)


def general(queries, keys, values, block_of_slot, doc_lengths, out_weight):
    tok_rows = queries.shape[0]
    head_size = queries.shape[1]
    half_rows = tok_rows // 2
    head_total = lax.axis_size("head")
    group_size = min(8, head_total)
    kv_start = lax.axis_index("head") // group_size * head_size
    own_keys = lax.dynamic_slice_in_dim(keys, kv_start, head_size, 1)
    own_values = lax.dynamic_slice_in_dim(values, kv_start, head_size, 1)
    count = doc_lengths.shape[0]
    before = jnp.arange(count)[None, :] <= jnp.arange(count - 1)[:, None]
    bounds = jnp.sum(jnp.where(before, doc_lengths[None, :], 0), axis=1)
    query_pos = slot_positions(lax.axis_index("dp") * tok_rows, tok_rows, block_of_slot, half_rows)
    query_doc = document_ids(query_pos, bounds)
    score_scale = 1.0 / math.sqrt(head_size)

    def attend(totals, key_block, value_block, allowed):
        run_max, run_sum, run_acc = totals
        scores = (
            jnp.einsum("qd,kd->qk", queries, key_block, preferred_element_type=jnp.float32)
            * score_scale
        )
        masked = jnp.where(allowed, scores, NEG)
        new_max = jnp.maximum(run_max, jnp.max(masked, axis=1))
        weights = jnp.where(allowed, jnp.exp(masked - new_max[:, None]), 0.0)
        factor = jnp.exp(run_max - new_max)
        new_sum = run_sum * factor + jnp.sum(weights, axis=1)
        new_acc = run_acc * factor[:, None] + jnp.dot(
            weights.astype(jnp.bfloat16), value_block, preferred_element_type=jnp.float32
        )
        return (new_max, new_sum, new_acc)

    totals = (
        jnp.full((tok_rows,), NEG, jnp.float32),
        jnp.zeros((tok_rows,), jnp.float32),
        jnp.zeros((tok_rows, head_size), jnp.float32),
    )
    key_piece = lax.all_gather(own_keys, "dp", axis=0, tiled=True)
    value_piece = lax.all_gather(own_values, "dp", axis=0, tiled=True)
    shard_count = key_piece.shape[0] // tok_rows
    per_step = max(
        [1]
        + [
            option_width
            for option_width in range(1, shard_count + 1)
            if shard_count % option_width == 0 and option_width * tok_rows <= 1536
        ]
    )
    step_rows = per_step * tok_rows
    step_count = shard_count // per_step
    key_blocks = key_piece.reshape(step_count, step_rows, head_size)
    value_blocks = value_piece.reshape(step_count, step_rows, head_size)
    step_starts = step_rows * jnp.arange(step_count, dtype=jnp.int32)

    def advance(running, inputs):
        key_block, value_block, block_start = inputs
        key_pos = slot_positions(block_start, step_rows, block_of_slot, half_rows)
        key_doc = document_ids(key_pos, bounds)
        allowed = (query_doc[:, None] == key_doc[None, :]) & (
            key_pos[None, :] <= query_pos[:, None]
        )
        running = lax.cond(
            jnp.any(allowed),
            lambda held: attend(held, key_block, value_block, allowed),
            lambda held: held,
            running,
        )
        return (running, None)

    totals, _ = lax.scan(advance, totals, (key_blocks, value_blocks, step_starts))
    run_max, run_sum, run_acc = totals
    attended = (run_acc / run_sum[:, None]).astype(jnp.bfloat16)
    partial_terms = jnp.dot(attended, out_weight, preferred_element_type=jnp.float32)
    return lax.psum_scatter(
        partial_terms.astype(jnp.bfloat16), "head", scatter_dimension=0, tiled=True
    )


def flip(index, bit):
    return index + bit - 2 * bit * lax.rem(lax.div(index, bit), 2)


def flipped(index, mask):
    bit = 1
    while bit <= mask:
        if mask & bit:
            index = flip(index, bit)
        bit *= 2
    return index


CORE, ALONG_X, ALONG_Y = 1, 2, 4
DIAG = ALONG_X + ALONG_Y


def fused_kernel(
    dp_total, head_total, shared, table, lengths, q_in, k_in, v_in, w_in, out_ref,
    q_buf, k_buf, v_buf, w_buf, att_buf,
    local_sem, q_send, q_recv, k_send, k_recv, v_send, v_recv, z_send, z_recv, w_send, w_recv, s_send, s_recv,
):
    me, head = lax.axis_index("dp"), lax.axis_index("head")
    rows, head_size = q_buf.shape[1:]
    tok_rows = k_buf.shape[1]
    half_rows = tok_rows // 2
    depth, width = w_buf.shape[1:]
    piece = width // dp_total
    near = {mask: flipped(me, mask) for mask in range(dp_total)}
    heads = {mask: flipped(head, mask) for mask in range(head_total)}

    barrier = pltpu.get_barrier_semaphore()
    for mask in (CORE, ALONG_X, ALONG_Y):
        pl.semaphore_signal(barrier, inc=1, device_id=(near[mask], head), device_id_type=MESH)
    for mask in range(1, head_total):
        pl.semaphore_signal(barrier, inc=1, device_id=(me, heads[mask]), device_id_type=MESH)

    def own_rows(of_head):
        return q_in.at[pl.ds(pl.multiple_of(of_head * rows, 16), rows)]

    locals_ = [
        pltpu.make_async_copy(k_in, k_buf.at[0], local_sem.at[0]),
        pltpu.make_async_copy(v_in, v_buf.at[0], local_sem.at[1]),
        pltpu.make_async_copy(own_rows(head), q_buf.at[0], local_sem.at[2]),
        pltpu.make_async_copy(w_in, w_buf.at[0], local_sem.at[3]),
    ]
    for copy in locals_:
        copy.start()
    for copy in locals_:
        copy.wait()
    pl.semaphore_wait(barrier, 3 + head_total - 1)

    sent = []

    def send(src, dst, send_sem, recv_sem, to):
        copy = pltpu.make_async_remote_copy(
            src_ref=src, dst_ref=dst, send_sem=send_sem, recv_sem=recv_sem,
            device_id=to, device_id_type=MESH,
        )
        copy.start()
        sent.append(copy)

    def arrived(dst, recv_sem):
        pltpu.make_async_remote_copy(
            src_ref=dst, dst_ref=dst, send_sem=recv_sem, recv_sem=recv_sem,
            device_id=(near[CORE], head), device_id_type=MESH,
        ).wait_recv()

    def pass_on(buf, send_sems, recv_sems, slot, mask, src=None):
        landing = slot ^ mask
        number = landing * 3 + (CORE, ALONG_X, ALONG_Y).index(mask)
        send(
            buf.at[slot] if src is None else src, buf.at[landing],
            send_sems.at[number], recv_sems.at[landing], (near[mask], head),
        )

    def k_pass(slot, mask, src=None):
        pass_on(k_buf, k_send, k_recv, slot, mask, src)

    def v_pass(slot, mask, src=None):
        pass_on(v_buf, v_send, v_recv, slot, mask, src)

    def k_wait(slot):
        arrived(k_buf.at[slot], k_recv.at[slot])

    def v_wait(slot):
        arrived(v_buf.at[slot], v_recv.at[slot])

    def columns_of(origin):
        return pl.ds(pl.multiple_of(near[origin] * piece, 128), piece)

    def w_part(foreign, origin, half):
        span = pl.ds(0, shared) if half is None else pl.ds(half * (shared // 2), shared // 2)
        return w_buf.at[foreign, span, columns_of(origin)]

    def w_number(origin, half):
        return origin if origin & DIAG != DIAG else dp_total + 2 * (origin & 1) + (half or 0)

    def w_pass(foreign, slot, mask, half=None):
        number = w_number(slot ^ mask, half)
        send(
            w_part(foreign, slot, half), w_part(foreign, slot, half),
            w_send.at[foreign, number * 3 + (CORE, ALONG_X, ALONG_Y).index(mask)],
            w_recv.at[foreign, number], (near[mask], head),
        )

    def w_wait(foreign, slot, half=None):
        arrived(w_part(foreign, slot, half), w_recv.at[foreign, w_number(slot, half)])

    def straight(of_core):
        half_span = (depth - shared) // 2
        return pl.ds(pl.multiple_of(shared + of_core * half_span, 16), half_span)

    def straight_to_core(foreign):
        part = w_buf.at[foreign, straight(lax.rem(me, 2))]
        arrived(part, s_recv.at[0, foreign])
        send(part, part, s_send.at[1, foreign], s_recv.at[1, foreign], (near[CORE], head))

    k_pass(0, ALONG_X)
    v_pass(0, ALONG_Y)
    for mask in range(1, head_total):
        send(
            w_part(0, 0, None), w_part(mask, 0, None),
            z_send.at[mask], z_recv.at[mask], (me, heads[mask]),
        )
    v_pass(0, ALONG_X)
    k_pass(0, ALONG_Y)
    k_pass(0, CORE)
    v_pass(0, CORE)
    for mask in range(1, head_total):
        send(own_rows(heads[mask]), q_buf.at[mask], q_send.at[mask], q_recv.at[mask], (me, heads[mask]))
    if shared < depth:
        span = straight(lax.rem(me, 2))
        for mask in range(1, head_total):
            send(
                w_buf.at[0, span], w_buf.at[mask, span],
                s_send.at[0, mask], s_recv.at[0, mask], (me, heads[mask]),
            )

    first_slot = me * 2 + lax.div(head * rows, half_rows)
    first_pos = table[first_slot] * half_rows + lax.rem(head * rows, half_rows)
    query_pos = first_pos + lax.broadcasted_iota(jnp.int32, (rows, 1), 0)
    low = jnp.zeros((rows, 1), jnp.int32)
    bound = jnp.int32(0)
    for i in range(lengths.shape[0] - 1):
        bound = bound + lengths[i]
        low = jnp.where(query_pos >= bound, bound, low)
    lane = lax.broadcasted_iota(jnp.int32, (1, tok_rows), 1)
    exponent = math.log2(math.e) / math.sqrt(head_size)
    total_rows = head_total * rows

    def scores_of(slot):
        start0 = table[near[slot] * 2] * half_rows
        start1 = table[near[slot] * 2 + 1] * half_rows - half_rows
        key_pos = lane + jnp.where(lane < half_rows, start0, start1)
        allowed = (key_pos <= query_pos) & (key_pos >= low)
        scores = lax.dot_general(
            q_buf[...].reshape(total_rows, head_size), k_buf[slot],
            (((1,), (1,)), ((), ())), preferred_element_type=jnp.float32,
        ).reshape(head_total, rows, tok_rows)
        return jnp.where(allowed[None], scores, NEG).reshape(total_rows, tok_rows)

    def fold(totals, slot):
        masked = scores_of(slot)
        top = jnp.max(masked, axis=1, keepdims=True)
        new_max = top if totals is None else jnp.maximum(totals[0], top)
        weights = jnp.exp2((masked - new_max) * exponent)
        added = jnp.sum(weights, axis=1, keepdims=True)
        product = jnp.dot(weights.astype(jnp.bfloat16), v_buf[slot], preferred_element_type=jnp.float32)
        if totals is None:
            return new_max, added, product
        factor = jnp.exp2((totals[0] - new_max) * exponent)
        return new_max, totals[1] * factor + added, totals[2] * factor + product

    foreign_heads = range(1, head_total)

    def w_spread(foreign):
        arrived(w_part(foreign, 0, None), z_recv.at[foreign])
        for mask in (ALONG_X, ALONG_Y, CORE):
            w_pass(foreign, 0, mask)

    def w_second(foreign):
        w_wait(foreign, ALONG_X)
        w_pass(foreign, ALONG_X, ALONG_Y, 0)
        w_pass(foreign, ALONG_X, CORE)
        w_wait(foreign, ALONG_Y)
        w_pass(foreign, ALONG_Y, ALONG_X, 1)
        w_pass(foreign, ALONG_Y, CORE)

    def w_third(foreign):
        for half in (0, 1):
            w_wait(foreign, DIAG, half)
            w_pass(foreign, DIAG, CORE, half)

    k_wait(ALONG_X)
    k_pass(ALONG_X, ALONG_Y)
    k_pass(ALONG_X, CORE)
    v_wait(ALONG_Y)
    v_pass(ALONG_Y, ALONG_X)
    v_pass(ALONG_Y, CORE)
    w_spread(1)
    v_wait(ALONG_X)
    v_pass(ALONG_X, CORE)
    k_wait(ALONG_Y)
    k_pass(ALONG_Y, CORE)
    for foreign in foreign_heads[1:]:
        w_spread(foreign)
    k_wait(DIAG)
    k_pass(DIAG, CORE)
    v_wait(DIAG)
    v_pass(DIAG, CORE)
    for mask in foreign_heads:
        arrived(q_buf.at[mask], q_recv.at[mask])
    slots = [0, ALONG_X, ALONG_Y, CORE, CORE + ALONG_X, CORE + ALONG_Y, DIAG, CORE + DIAG]
    totals = None
    for slot in slots:
        if slot & CORE:
            k_wait(slot)
            v_wait(slot)
        totals = fold(totals, slot)
        number = slots.index(slot)
        if number % 2 and number // 2 < len(foreign_heads):
            w_second(foreign_heads[number // 2])
    for foreign in foreign_heads[(len(slots) // 2) :]:
        w_second(foreign)
    if shared < depth:
        for foreign in foreign_heads:
            straight_to_core(foreign)
    _, run_sum, run_acc = totals
    attended = (run_acc / run_sum).astype(jnp.bfloat16)
    for mask in range(head_total):
        att_buf[:, mask * head_size : (mask + 1) * head_size] = attended[mask * rows : (mask + 1) * rows]
    if shared < depth:
        for foreign in foreign_heads:
            arrived(w_buf.at[foreign, straight(1 - lax.rem(me, 2))], s_recv.at[1, foreign])

    def project(slot):
        columns = columns_of(slot)
        out_ref[:, columns] = jnp.dot(
            att_buf[...], w_buf[:, :, columns].reshape(head_total * depth, piece),
            preferred_element_type=jnp.float32,
        ).astype(out_ref.dtype)

    project(0)
    project(ALONG_X)
    project(ALONG_Y)
    for foreign in foreign_heads:
        w_third(foreign)
    for slot in (CORE, CORE + ALONG_X, CORE + ALONG_Y):
        for foreign in foreign_heads:
            w_wait(foreign, slot)
        project(slot)
    project(DIAG)
    for foreign in foreign_heads:
        w_wait(foreign, CORE + DIAG, 0)
        w_wait(foreign, CORE + DIAG, 1)
    project(CORE + DIAG)
    for copy in sent:
        copy.wait_send()


def fused(dp_total, head_total, queries, keys, values, block_of_slot, doc_lengths, out_weight):
    tok_rows, head_size = queries.shape
    rows = tok_rows // head_total
    depth, width = out_weight.shape
    any_, smem, vmem = (pl.BlockSpec(memory_space=m) for m in (pl.ANY, pltpu.SMEM, pltpu.VMEM))
    dma = pltpu.SemaphoreType.DMA
    shared = depth * 3 // 4 // 32 * 32
    return pl.pallas_call(
        functools.partial(fused_kernel, dp_total, head_total, shared),
        out_shape=jax.ShapeDtypeStruct((rows, width), jnp.bfloat16),
        in_specs=[smem, smem, any_, any_, any_, any_],
        out_specs=vmem,
        scratch_shapes=[
            pltpu.VMEM((head_total, rows, head_size), jnp.bfloat16),
            pltpu.VMEM((dp_total, tok_rows, head_size), jnp.bfloat16),
            pltpu.VMEM((dp_total, tok_rows, head_size), jnp.bfloat16),
            pltpu.VMEM((head_total, depth, width), jnp.bfloat16),
            pltpu.VMEM((rows, head_total * head_size), jnp.bfloat16),
            dma((4,)),
            dma((head_total,)),
            dma((head_total,)),
            dma((3 * dp_total,)),
            dma((dp_total,)),
            dma((3 * dp_total,)),
            dma((dp_total,)),
            dma((head_total,)),
            dma((head_total,)),
            dma((head_total, 3 * (dp_total + 4))),
            dma((head_total, dp_total + 4)),
            dma((2, head_total)),
            dma((2, head_total)),
        ],
        compiler_params=pltpu.CompilerParams(
            collective_id=0, has_side_effects=True, vmem_limit_bytes=60 * 2**20
        ),
        cost_estimate=pl.CostEstimate(
            flops=4 * tok_rows * tok_rows * dp_total * head_size + 2 * rows * head_total * depth * width,
            bytes_accessed=2 * (rows * width + depth * width + 3 * tok_rows * head_size),
            transcendentals=tok_rows * tok_rows * dp_total,
        ),
    )(
        block_of_slot, doc_lengths, queries, keys, values, out_weight,
    )


def solution(mesh):
    dp_total, head_total = mesh.shape["dp"], mesh.shape["head"]

    def per_device(queries, keys, values, block_of_slot, doc_lengths, out_weight):
        tok_rows, head_size = queries.shape
        rows = tok_rows // head_total
        fits = (
            dp_total == 2 ** 3
            and head_total & (head_total - 1) == 0
            and keys.shape[1] == head_size
            and rows % 16 == 0
            and (tok_rows // 2) % rows == 0
            and out_weight.shape[0] % 128 == 0
            and out_weight.shape[1] % (128 * dp_total) == 0
            and out_weight.shape[0] == head_size
        )
        run = functools.partial(fused, dp_total, head_total) if fits else general
        return run(queries, keys, values, block_of_slot, doc_lengths, out_weight)

    return jax.shard_map(
        per_device,
        mesh=mesh,
        in_specs=(P("dp", "head"), P("dp", None), P("dp", None), P(), P(), P("head", None)),
        out_specs=P(("dp", "head"), None),
        check_vma=False,
    )
```
